256 devices in a mesh: gx: 16 (over y, x), gy: 16 (over z, core).
Axes of the slice: x: 4, y: 4, z: 8, core: 2. Of those that a mesh axis runs over, the one named last changes fastest.
Arguments:
- charges: bfloat16 [16, 16, 512, 256], P('gx', 'gy'), may hold values from -6 to 6
- near_blocks: bfloat16 [16, 16, 3, 3, 512, 512], P('gx', 'gy'), may hold values from -0.09375 to 0.09375
- basis: bfloat16 [16, 16, 512, 128], P('gx', 'gy'), may hold values from -0.25 to 0.25
- transfer: bfloat16 [16, 16, 128, 128], P('gx', 'gy'), may hold values from -0.25 to 0.25
- coupling_leaf: bfloat16 [16, 16, 27, 128, 128], P('gx', 'gy'), may hold values from -0.109375 to 0.109375
- coupling_top: bfloat16 [16, 16, 27, 32, 128], P('gx', 'gy'), may hold values from -0.109375 to 0.109375
Outputs:
- potentials: bfloat16 [16, 16, 512, 256], P('gx', 'gy')
The draws below stay inside these ranges and needn't reach their ends.
All inputs are finite; a program needn't handle non-finite values.
Results may differ from the reference program's by a relative error of at most 0.0085.
Values may be sent and summed in bfloat16 or wider, within the bound.
A program may use at most 128 MiB of HBM per device.

```python
import jax
import jax.numpy as jnp
import numpy as np

LEAF = 512
RANK = 128
NRHS = 256
SLOTS = 27
NGX = 16
NGY = 16
QUART = 32


def levels(own_key, dims, pieces, least, top_value):
    loudness, own = 1.0, jax.random.fold_in(own_key, 6)
    for axis_at, blocks in pieces:
        draws = jnp.exp(jax.random.uniform(jax.random.fold_in(own, axis_at), (blocks,), jnp.float32, least / len(pieces), top_value / len(pieces)))
        loudness = loudness * jnp.repeat(draws, dims[axis_at] // blocks).reshape([-1 if axis == axis_at else 1 for axis in range(len(dims))])
    return loudness


def centred(rng, dims, spread, bound, cuts=(), dtype=jnp.bfloat16):
    entries = jax.random.normal(rng, dims, jnp.float32) * spread
    if len(cuts) > 0:
        entries = levels(rng, dims, cuts, -0.22, 0.18) * entries
    return jnp.clip(entries, min=-bound, max=bound).astype(dtype)


def setup_inputs(seed: int = 0) -> dict:
    streams_of = jax.random.split(jax.random.key(seed), 7)
    charges = centred(streams_of[0], (NGX, NGY, LEAF, NRHS), 1.0, 6.0, ((0, 16), (1, 16)))
    near_blocks = centred(streams_of[1], (NGX, NGY, 3, 3, LEAF, LEAF), (9 * LEAF) ** -0.5, 0.09375, ((0, 16), (1, 16)))
    basis = centred(streams_of[2], (NGX, NGY, LEAF, RANK), LEAF ** -0.5, 0.25, ((0, 16), (1, 16)))
    transfer = centred(streams_of[3], (NGX, NGY, RANK, RANK), (4 * RANK) ** -0.5, 0.25, ((0, 16), (1, 16)))
    coupling_leaf = centred(streams_of[4], (NGX, NGY, SLOTS, RANK, RANK), (SLOTS * RANK) ** -0.5, 0.109375, ((0, 16), (1, 16)))
    coupling_top = centred(streams_of[5], (NGX, NGY, SLOTS, QUART, RANK), (SLOTS * RANK) ** -0.5, 0.109375, ((0, 16), (1, 16)))
    return dict(charges=charges, near_blocks=near_blocks, basis=basis, transfer=transfer, coupling_leaf=coupling_leaf, coupling_top=coupling_top)


def cousin_table():
    table = np.zeros((2, 2, 27), np.int32)
    for parity_a in range(2):
        for parity_b in range(2):
            slot = 0
            for big_a in range(6):
                for big_b in range(6):
                    off_a = big_a - 2 - parity_a
                    off_b = big_b - 2 - parity_b
                    if abs(off_a) <= 1 and abs(off_b) <= 1:
                        continue
                    table[parity_a, parity_b, slot] = (off_a + 3) * 7 + (off_b + 3)
                    slot += 1
    return table


def cousin_sources(grid):
    rows_n, cols_n = grid.shape[0], grid.shape[1]
    padded = jnp.pad(grid, ((3, 3), (3, 3), (0, 0), (0, 0)))
    table = cousin_table()
    index_a = np.arange(rows_n)[:, None] + np.zeros((1, cols_n), np.int32)
    index_b = np.arange(cols_n)[None, :] + np.zeros((rows_n, 1), np.int32)
    flat = table[index_a % 2, index_b % 2]
    where_a = (index_a[:, :, None] + flat // 7).astype(np.int32)
    where_b = (index_b[:, :, None] + flat % 7).astype(np.int32)
    return padded[where_a, where_b]


def reference(charges, near_blocks, basis, transfer, coupling_leaf, coupling_top):
    f32 = jnp.float32
    rows_n, cols_n = charges.shape[0], charges.shape[1]
    rank_n = basis.shape[3]
    moments = jnp.einsum('abjk,abjn->abkn', basis.astype(f32), charges.astype(f32)).astype(jnp.bfloat16)
    terms = jnp.einsum('abrk,abrn->abkn', transfer.astype(f32), moments.astype(f32))
    top = terms.reshape(rows_n // 2, 2, cols_n // 2, 2, rank_n, -1).sum((1, 3)).astype(jnp.bfloat16)
    local_leaf = jnp.einsum('abskr,absrn->abkn', coupling_leaf.astype(f32), cousin_sources(moments).astype(f32))
    full_top = coupling_top.reshape(rows_n // 2, 2, cols_n // 2, 2, 27, rank_n // 4, rank_n)
    full_top = full_top.transpose(0, 2, 4, 1, 3, 5, 6).reshape(rows_n // 2, cols_n // 2, 27, rank_n, rank_n)
    local_top = jnp.einsum('abskr,absrn->abkn', full_top.astype(f32), cousin_sources(top).astype(f32)).astype(jnp.bfloat16)
    parent = jnp.repeat(jnp.repeat(local_top, 2, 0), 2, 1)
    total = (local_leaf + jnp.einsum('abkr,abrn->abkn', transfer.astype(f32), parent.astype(f32))).astype(jnp.bfloat16)
    padded = jnp.pad(charges, ((1, 1), (1, 1), (0, 0), (0, 0))).astype(f32)
    near_sum = jnp.zeros(charges.shape, f32)
    for step_u in range(3):
        for step_v in range(3):
            near_sum = near_sum + jnp.einsum('abij,abjn->abin', near_blocks[:, :, step_u, step_v].astype(f32), padded[step_u:step_u + rows_n, step_v:step_v + cols_n])
    far_sum = jnp.einsum('abjk,abkn->abjn', basis.astype(f32), total.astype(f32))
    return (near_sum + far_sum).astype(jnp.bfloat16)
```

```python
import jax
import jax.numpy as jnp
from jax import lax
from jax.experimental import pallas as pl
from jax.experimental.pallas import tpu as pltpu
from jax.sharding import PartitionSpec as P

F32, BF16 = jnp.float32, jnp.bfloat16
SLOTS, ROWS, LEAF, NRHS, RANK = 27, 16, 512, 256, 128
PART = NRHS // 4
TILE = 256


def cousin_positions():
    table = {}
    for i in range(2):
        for j in range(2):
            table[i, j] = [
                (big_a, big_b)
                for big_a in range(6)
                for big_b in range(6)
                if not (abs(big_a - 2 - i) <= 1 and abs(big_b - 2 - j) <= 1)
            ]
    return table


POSITIONS = cousin_positions()


def pick(value, i, j):
    v00, v01, v10, v11 = (value[0, 0], value[0, 1], value[1, 0], value[1, 1])
    return v00 + i * (v10 - v00) + j * (v01 - v00) + i * j * (v11 - v10 - v01 + v00)


def place(slot, i, j):
    big_a = pick({k: t[slot][0] for k, t in POSITIONS.items()}, i, j)
    big_b = pick({k: t[slot][1] for k, t in POSITIONS.items()}, i, j)
    return big_a, big_b


def dot(a, b, contract):
    return lax.dot_general(a, b, ((contract[:1], contract[1:]), ((), ())), preferred_element_type=F32)


def kernel(
    x_hbm, near_hbm, basis_hbm, transfer_hbm, leaf_hbm, top_hbm, out_hbm,
    near, basis, transfer, cl, ct, n, w, term, rb, t, lt, acc, out,
    local_sem, send_sem, recv_sem,
):
    a, b = lax.axis_index("gx"), lax.axis_index("gy")
    y, x = a // 4, a % 4
    z, c = b // 2, b % 2
    xh, alpha = x // 2, x % 2
    zz, zp = z // 2, z % 2
    mine = 2 * alpha + c

    def device(y, x, z, c):
        return (y * 4 + x, z * 2 + c)

    def flip(v, by):
        high, low = v // 2, v % 2
        return 2 * ((high + by // 2) % 2) + (low + by % 2) % 2

    locals_ = []

    def local(src, dst):
        copy = pltpu.make_async_copy(src, dst, local_sem.at[len(locals_)])
        copy.start()
        locals_.append(copy)
        return copy

    load_x = local(x_hbm.at[0, 0], n.at[4])
    load_basis = local(basis_hbm.at[0, 0], basis)
    load_transfer = local(transfer_hbm.at[0, 0], transfer)
    my_rows = pl.ds(pl.multiple_of(mine * 32, 32), 32)
    load_ct = local(top_hbm.at[0, 0], ct.at[:, my_rows, :])
    load_cl = local(leaf_hbm.at[0, 0], cl)
    load_near = local(near_hbm.at[0, 0], near)

    ring = [(dx, dc) for dx in range(4) for dc in range(2) if (dx, dc) != (0, 0)]
    ring_device = {k: device(y, flip(x, k[0]), z, (c + k[1]) % 2) for k in ring}
    up_y, down_y = device((y + 1) % 4, x, z, c), device((y + 3) % 4, x, z, c)
    window = [(e, g) for e in (-1, 0, 1) for g in range(2) if (e, g) != (0, 0)]
    window_device = {
        (e, g): device(y, x, 2 * ((zz + 4 + e) % 4) + (zp + g) % 2, c) for e, g in window
    }
    next_a, prev_a = ((a + 1) % 16, b), ((a + 15) % 16, b)
    next_b, prev_b = (a, (b + 1) % 16), (a, (b + 15) % 16)
    next_z, prev_z = device(y, x, (z + 1) % 8, c), device(y, x, (z + 7) % 8, c)
    greeted = (
        [ring_device[k] for k in ring]
        + [up_y, down_y]
        + [window_device[k] for k in window]
        + [next_a, prev_a, next_b, prev_b, next_z, prev_z]
    )
    barrier = pltpu.get_barrier_semaphore()
    for partner in greeted:
        pl.semaphore_signal(barrier, inc=1, device_id=partner, device_id_type=pl.DeviceIdType.MESH)

    sent = []

    def send(src, dst, to):
        k = len(sent)
        copy = pltpu.make_async_remote_copy(
            src_ref=src, dst_ref=dst, send_sem=send_sem.at[k], recv_sem=recv_sem.at[k],
            device_id=to, device_id_type=pl.DeviceIdType.MESH,
        )
        copy.start()
        sent.append(copy)
        return copy

    n[9] = jnp.zeros((LEAF, NRHS), BF16)
    w[12, 0] = jnp.zeros((RANK, NRHS), BF16)
    t[6, 0] = jnp.zeros((PART, RANK), BF16)

    load_x.wait()
    load_basis.wait()
    moments = dot(basis[...], n[4], (0, 0)).astype(BF16)
    own_row = c * 6 + 2 + alpha
    w[own_row, 1] = moments
    load_transfer.wait()
    terms = dot(moments, transfer[...], (0, 0)).astype(BF16)
    term[...] = terms.reshape(4, PART, RANK)
    rb[xh, mine] = term[mine]
    load_ct.wait()

    pl.semaphore_wait(barrier, len(greeted))

    top_term = [
        send(
            term.at[2 * ((alpha + dx % 2) % 2) + (c + dc) % 2],
            rb.at[xh, mine],
            ring_device[dx, dc],
        )
        for dx, dc in ring
    ]
    moments_z = [
        send(w.at[own_row, 1], w.at[own_row, 0], next_z),
        send(w.at[own_row, 1], w.at[own_row, 2], prev_z),
    ]
    charges_b = [send(n.at[4], n.at[3], next_b), send(n.at[4], n.at[5], prev_b)]
    charges_a = [send(n.at[4], n.at[1], next_a), send(n.at[4], n.at[7], prev_a)]
    quarter_c = send(ct.at[:, my_rows, :], ct.at[:, my_rows, :], ring_device[0, 1])
    quarter_x = send(ct.at[:, my_rows, :], ct.at[:, my_rows, :], ring_device[1, 0])

    def charge_at(u, v):
        va, vb = a + u - 1, b + v - 1
        inside = (va >= 0) & (va < 16) & (vb >= 0) & (vb < 16)
        return jnp.where(inside, 3 * u + v, 9)

    def near_add(blocks, first=False):
        @pl.loop(0, LEAF // TILE)
        def _(i):
            rows = pl.ds(pl.multiple_of(i * TILE, TILE), TILE)
            total = None if first else acc[rows, :]
            for u, v in blocks:
                product = dot(near[u, v, rows, :], n[charge_at(u, v)], (1, 0))
                total = product if total is None else total + product
            acc[rows, :] = total

    load_near.wait()
    near_add([(1, 1)], first=True)

    for copy in top_term:
        copy.wait_recv()
    for h in range(2):
        total = rb[h, 0].astype(F32)
        for j in range(1, 4):
            total = total + rb[h, j].astype(F32)
        t[2 + zp, 2 + h] = total.astype(BF16)
    top_z = [
        send(t.at[2 + zp, pl.ds(2, 2)], t.at[2 - 2 * e + zp, pl.ds(2, 2)], window_device[e, g])
        for e, g in window
    ]

    for copy in moments_z:
        copy.wait_recv()
    moments_x = []
    for dx in (1, 2, 3):
        far = (xh + dx // 2) % 2
        moments_x.append(
            send(w.at[own_row], w.at[c * 6 + x + 2 * (1 - far)], ring_device[dx, 0])
        )
    moments_c = [send(w.at[own_row], w.at[own_row], ring_device[0, 1])]

    for copy in top_z:
        copy.wait_recv()
    top_y = [
        send(t.at[pl.ds(0, 6), pl.ds(2, 2)], t.at[pl.ds(0, 6), pl.ds(0, 2)], up_y),
        send(t.at[pl.ds(0, 6), pl.ds(2, 2)], t.at[pl.ds(0, 6), pl.ds(4, 2)], down_y),
    ]

    corners = []
    for u, copy in zip((0, 2), charges_a):
        copy.wait_recv()
        corners.append(send(n.at[3 * u + 1], n.at[3 * u], next_b))
        corners.append(send(n.at[3 * u + 1], n.at[3 * u + 2], prev_b))
    near_add([(0, 1), (2, 1)])

    for dx, copy in zip((1, 2, 3), moments_x):
        copy.wait_recv()
    send_to = (((y + 1 + 2 * xh) % 4) * 4 + x, b)
    moments_y = send(
        w.at[pl.ds(c * 6 + 4 - 4 * xh, 2)], w.at[pl.ds(c * 6 + 4 * xh, 2)], send_to
    )
    for dx in (1, 2, 3):
        row = c * 6 + flip(x, dx) + 2 * (1 - xh)
        moments_c.append(send(w.at[row], w.at[row], ring_device[0, 1]))

    quarter_c.wait_recv()
    quarter_x.wait_recv()
    other_rows = pl.ds(pl.multiple_of((2 * (1 - alpha) + c) * 32, 32), 32)
    quarter_d = send(ct.at[:, other_rows, :], ct.at[:, other_rows, :], ring_device[0, 1])

    for copy in charges_b:
        copy.wait_recv()
    near_add([(1, 0), (1, 2)])

    quarter_d.wait_recv()
    for copy in top_y:
        copy.wait_recv()
    quarter = None
    for s in range(SLOTS):
        big_p, big_q = place(s, xh, zp)
        vp, vq = 2 * y - 2 + big_p, 2 * zz - 2 + big_q
        inside = (vp >= 0) & (vp < 8) & (vq >= 0) & (vq < 8)
        box = t[jnp.where(inside, big_q, 6), jnp.where(inside, big_p, 0)]
        product = dot(box, ct[s], (1, 1))
        quarter = product if quarter is None else quarter + product
    lt[mine] = quarter.astype(BF16)
    siblings = [(0, 1), (1, 0), (1, 1)]
    expansion = [send(lt.at[mine], lt.at[mine], ring_device[k]) for k in siblings]

    moments_y.wait_recv()
    rows_y = pl.ds(c * 6 + 4 * xh, 2)
    moments_c.append(send(w.at[rows_y], w.at[rows_y], ring_device[0, 1]))

    for copy in corners:
        copy.wait_recv()
    near_add([(0, 0), (0, 2), (2, 0), (2, 2)])

    load_cl.wait()
    for copy in moments_c:
        copy.wait_recv()
    local_leaf = None
    for s in range(SLOTS):
        big_a, big_b = place(s, alpha, c)
        va, vb = a - alpha - 2 + big_a, b - c - 2 + big_b
        inside = (va >= 0) & (va < 16) & (vb >= 0) & (vb < 16)
        row = jnp.where(inside, (big_b % 2) * 6 + big_a, 12)
        product = dot(cl[s], w[row, jnp.where(inside, big_b // 2, 0)], (1, 0))
        local_leaf = product if local_leaf is None else local_leaf + product

    for copy in expansion:
        copy.wait_recv()
    full = lt[...].reshape(NRHS, RANK)
    total = (local_leaf + dot(transfer[...], full, (1, 1))).astype(BF16)
    stores = []
    for i in range(LEAF // TILE):
        rows = pl.ds(i * TILE, TILE)
        out[rows, :] = (acc[rows, :] + dot(basis[rows, :], total, (1, 0))).astype(BF16)
        stores.append(local(out.at[rows, :], out_hbm.at[0, 0, rows, :]))

    for copy in sent:
        copy.wait_send()
    for copy in stores:
        copy.wait()


def shards(charges, near_blocks, basis, transfer, coupling_leaf, coupling_top):
    any_space = pl.BlockSpec(memory_space=pl.ANY)
    return pl.pallas_call(
        kernel,
        out_shape=jax.ShapeDtypeStruct((1, 1, LEAF, NRHS), BF16),
        in_specs=[any_space] * 6,
        out_specs=any_space,
        scratch_shapes=[
            pltpu.VMEM((3, 3, LEAF, LEAF), BF16),
            pltpu.VMEM((LEAF, RANK), BF16),
            pltpu.VMEM((RANK, RANK), BF16),
            pltpu.VMEM((SLOTS, RANK, RANK), BF16),
            pltpu.VMEM((SLOTS, RANK, RANK), BF16),
            pltpu.VMEM((10, LEAF, NRHS), BF16),
            pltpu.VMEM((13, 3, RANK, NRHS), BF16),
            pltpu.VMEM((4, PART, RANK), BF16),
            pltpu.VMEM((2, 4, PART, RANK), BF16),
            pltpu.VMEM((7, 6, PART, RANK), BF16),
            pltpu.VMEM((4, PART, RANK), BF16),
            pltpu.VMEM((LEAF, NRHS), F32),
            pltpu.VMEM((LEAF, NRHS), BF16),
            pltpu.SemaphoreType.DMA((8,)),
            pltpu.SemaphoreType.DMA((48,)),
            pltpu.SemaphoreType.DMA((48,)),
        ],
        compiler_params=pltpu.CompilerParams(
            collective_id=0, has_side_effects=True, vmem_limit_bytes=48 * 1024 * 1024
        ),
        cost_estimate=pl.CostEstimate(
            flops=1_600_000_000, bytes_accessed=6_500_000, transcendentals=0
        ),
    )(charges, near_blocks, basis, transfer, coupling_leaf, coupling_top)


def solution(mesh):
    return jax.shard_map(
        shards,
        mesh=mesh,
        in_specs=(
            P("gx", "gy", None, None),
            P("gx", "gy", None, None, None, None),
            P("gx", "gy", None, None),
            P("gx", "gy", None, None),
            P("gx", "gy", None, None, None),
            P("gx", "gy", None, None, None),
        ),
        out_specs=P("gx", "gy", None, None),
        check_vma=False,
    )
```

```python
import jax
import jax.numpy as jnp
from jax import lax
from jax.experimental import pallas as pl
from jax.experimental.pallas import tpu as pltpu
from jax.sharding import PartitionSpec as P

F32, BF16 = jnp.float32, jnp.bfloat16
SLOTS, ROWS, LEAF, NRHS, RANK = 27, 16, 512, 256, 128
PART = NRHS // 4
TILE = 256


def cousin_positions():
    table = {}
    for i in range(2):
        for j in range(2):
            table[i, j] = [
                (big_a, big_b)
                for big_a in range(6)
                for big_b in range(6)
                if not (abs(big_a - 2 - i) <= 1 and abs(big_b - 2 - j) <= 1)
            ]
    return table


POSITIONS = cousin_positions()


def pick(value, i, j):
    v00, v01, v10, v11 = (value[0, 0], value[0, 1], value[1, 0], value[1, 1])
    return v00 + i * (v10 - v00) + j * (v01 - v00) + i * j * (v11 - v10 - v01 + v00)


def place(slot, i, j):
    big_a = pick({k: t[slot][0] for k, t in POSITIONS.items()}, i, j)
    big_b = pick({k: t[slot][1] for k, t in POSITIONS.items()}, i, j)
    return big_a, big_b


def dot(a, b, contract):
    return lax.dot_general(a, b, ((contract[:1], contract[1:]), ((), ())), preferred_element_type=F32)


class Copy:
    def __init__(self, make, goes, comes):
        self.make, self.goes, self.comes = make, goes, comes

    def _if(self, condition, act):
        if condition is True:
            act()
        else:
            pl.when(condition)(act)

    def start(self):
        self._if(self.goes, lambda: self.make().start())

    def wait_recv(self):
        self._if(self.comes, lambda: self.make().wait_recv())

    def wait_send(self):
        self._if(self.goes, lambda: self.make().wait_send())


def both(p, q):
    return q if p is True else p if q is True else p & q


def kernel(
    x_hbm, near_hbm, basis_hbm, transfer_hbm, leaf_hbm, top_hbm, out_hbm,
    near, basis, transfer, cl, ct, n, w, term, rb, t, lt, acc, out,
    local_sem, send_sem, recv_sem,
):
    a, b = lax.axis_index("gx"), lax.axis_index("gy")
    y, x = a // 4, a % 4
    z, c = b // 2, b % 2
    xh, alpha = x // 2, x % 2
    zz, zp = z // 2, z % 2
    mine = 2 * alpha + c

    def device(y, x, z, c):
        return (y * 4 + x, z * 2 + c)

    def flip(v, by):
        high, low = v // 2, v % 2
        return 2 * ((high + by // 2) % 2) + (low + by % 2) % 2

    locals_ = []

    def local(src, dst):
        copy = pltpu.make_async_copy(src, dst, local_sem.at[len(locals_)])
        copy.start()
        locals_.append(copy)
        return copy

    ring = [(dx, dc) for dx in (1, 3, 2, 0) for dc in range(2) if (dx, dc) != (0, 0)]
    ring_device = {k: device(y, flip(x, k[0]), z, (c + k[1]) % 2) for k in ring}
    core = ring_device[0, 1]
    up, down = y < 3, y > 0
    up_y, down_y = device((y + 1) % 4, x, z, c), device((y + 3) % 4, x, z, c)
    over = ((xh == 1) & up) | ((xh == 0) & down)
    over_device = [
        device((y + 3 + 2 * xh) % 4, flip(x, 2 + g), z, c) for g in range(2)
    ]
    window = [(0, 1), (-1, 0), (-1, 1), (1, 0), (1, 1)]
    window_device = {
        (e, g): device(y, x, 2 * ((zz + 4 + e) % 4) + (zp + g) % 2, c) for e, g in window
    }
    window_goes = {-1: zz > 0, 0: True, 1: zz < 3}
    window_comes = {-1: zz < 3, 0: True, 1: zz > 0}
    next_a, prev_a = ((a + 1) % 16, b), ((a + 15) % 16, b)
    next_b, prev_b = (a, (b + 1) % 16), (a, (b + 15) % 16)
    next_z, prev_z = device(y, x, (z + 1) % 8, c), device(y, x, (z + 7) % 8, c)
    far_b = device(y, x, (z + 7 + 2 * c) % 8, 1 - c)
    far = ((c == 1) & (z < 7)) | ((c == 0) & (z > 0))

    barrier = pltpu.get_barrier_semaphore()

    def greet(partners):
        for partner in partners:
            pl.semaphore_signal(
                barrier, inc=1, device_id=partner, device_id_type=pl.DeviceIdType.MESH
            )

    pl.when(zz > 0)(lambda: greet([window_device[-1, 0], window_device[-1, 1]]))
    pl.when(zz < 3)(lambda: greet([window_device[1, 0], window_device[1, 1]]))
    greet([window_device[0, 1]])
    pl.when(up)(lambda: greet([up_y]))
    pl.when(down)(lambda: greet([down_y]))
    pl.when(over)(lambda: greet(over_device))
    pl.when(far)(lambda: greet([far_b]))
    greet([ring_device[k] for k in ring])

    def one(condition):
        return jnp.where(condition, 1, 0)

    expected = (
        8 + 2 * one(zz > 0) + 2 * one(zz < 3) + one(up) + one(down) + 2 * one(over) + one(far)
    )

    load_x = local(x_hbm.at[0, 0], n.at[4])
    load_basis = local(basis_hbm.at[0, 0], basis)
    load_transfer = local(transfer_hbm.at[0, 0], transfer)
    my_rows = pl.ds(pl.multiple_of(mine * 32, 32), 32)
    load_ct = local(top_hbm.at[0, 0], ct.at[:, my_rows, :])
    load_near = local(near_hbm.at[0, 0], near)
    load_cl = local(leaf_hbm.at[0, 0], cl)

    sent = []

    def send(kind, src, dst, to, goes=True, comes=True):
        k = len(sent)
        copy = Copy(
            lambda: pltpu.make_async_remote_copy(
                src_ref=src, dst_ref=dst, send_sem=send_sem.at[k], recv_sem=recv_sem.at[k],
                device_id=to, device_id_type=pl.DeviceIdType.MESH,
            ),
            goes,
            comes,
        )
        copy.start()
        sent.append(copy)
        return copy

    n[9] = jnp.zeros((LEAF, NRHS), BF16)
    w[12, 0] = jnp.zeros((RANK, NRHS), BF16)
    t[6, 0] = jnp.zeros((PART, RANK), BF16)

    load_x.wait()
    load_basis.wait()
    moments = dot(basis[...], n[4], (0, 0)).astype(BF16)
    own = 2 + alpha
    w[c * 6 + own, 1] = moments
    load_transfer.wait()
    terms = dot(moments, transfer[...], (0, 0)).astype(BF16)
    term[...] = terms.reshape(4, PART, RANK)
    rb[xh, mine] = term[mine]
    load_ct.wait()

    pl.semaphore_wait(barrier, expected)

    top_term = [
        send(
            "top",
            term.at[2 * ((alpha + dx % 2) % 2) + (c + dc) % 2],
            rb.at[xh, mine],
            ring_device[dx, dc],
        )
        for dx, dc in ring
    ]
    center = w.at[c * 6 + own, 1]
    came_from = []
    for dx in (1, 3, 2):
        far_h = (xh + dx // 2) % 2
        copy = send("mom", center, w.at[c * 6 + x + 2 * (1 - far_h), 1], ring_device[dx, 0])
        came_from.append((flip(x, dx) + 2 * (1 - xh), copy, True))
    for g in range(2):
        copy = send(
            "mom", center, w.at[c * 6 + alpha + 4 * (1 - xh), 1], over_device[g], over, over
        )
        came_from.append(((alpha + g) % 2 + 4 * xh, copy, over))

    to_core = []

    def along_z(row, there):
        place_ = c * 6 + row
        return (
            row,
            there,
            send("mom", w.at[place_, 1], w.at[place_, 0], next_z, both(there, z < 7), both(there, z > 0)),
            send("mom", w.at[place_, 1], w.at[place_, 2], prev_z, both(there, z > 0), both(there, z < 7)),
        )

    def across(row, there, from_prev, from_next):
        from_prev.wait_recv()
        from_next.wait_recv()
        place_ = c * 6 + row
        to_core.append(send("mom", w.at[place_], w.at[place_], core, there, there))

    came_z = [along_z(own, True)]
    charges_b = [
        send("cha", n.at[4], n.at[3], next_b, b < 15, b > 0),
        send("cha", n.at[4], n.at[5], prev_b, b > 0, b < 15),
    ]
    halves = [pl.ds(h * LEAF // 2, LEAF // 2) for h in range(2)]
    charges_a = [
        (
            half,
            send("cha", n.at[4, half], n.at[1, half], next_a, a < 15, a > 0),
            send("cha", n.at[4, half], n.at[7, half], prev_a, a > 0, a < 15),
        )
        for half in halves
    ]
    quarter_c = send("ctg", ct.at[:, my_rows, :], ct.at[:, my_rows, :], core)
    quarter_x = send("ctg", ct.at[:, my_rows, :], ct.at[:, my_rows, :], ring_device[1, 0])

    def charge_at(u, v):
        va, vb = a + u - 1, b + v - 1
        inside = (va >= 0) & (va < 16) & (vb >= 0) & (vb < 16)
        return jnp.where(inside, 3 * u + v, 9)

    def near_add(blocks, first=False):
        @pl.loop(0, LEAF // TILE)
        def _(i):
            rows = pl.ds(pl.multiple_of(i * TILE, TILE), TILE)
            total = None if first else acc[rows, :]
            for u, v in blocks:
                product = dot(near[u, v, rows, :], n[charge_at(u, v)], (1, 0))
                total = product if total is None else total + product
            acc[rows, :] = total

    for copy in top_term:
        copy.wait_recv()
    for h in range(2):
        total = rb[h, 0].astype(F32)
        for j in range(1, 4):
            total = total + rb[h, j].astype(F32)
        t[2 + zp, 2 + h] = total.astype(BF16)
    top_z = {
        (e, g): send(
            "top",
            t.at[2 + zp, pl.ds(2, 2)],
            t.at[2 - 2 * e + zp, pl.ds(2, 2)],
            window_device[e, g],
            window_goes[e],
            window_comes[e],
        )
        for e, g in window
    }

    for row, copy, there in came_from[:3]:
        copy.wait_recv()
        came_z.append(along_z(row, there))

    load_near.wait()
    near_add([(1, 1)], first=True)

    top_y = []

    def along_y(pair, there):
        columns = pl.ds(2 * pair, 2)
        for rows, to, goes, comes in ((0, up_y, up, down), (4, down_y, down, up)):
            top_y.append(
                send(
                    "top",
                    t.at[columns, pl.ds(2, 2)],
                    t.at[columns, pl.ds(rows, 2)],
                    to,
                    both(there, goes),
                    both(there, comes),
                )
            )

    top_z[0, 1].wait_recv()
    along_y(1, True)
    for row, copy, there in came_from[3:]:
        copy.wait_recv()
        came_z.append(along_z(row, there))
    for e in (-1, 1):
        top_z[e, 0].wait_recv()
        top_z[e, 1].wait_recv()
        along_y(1 - e, window_comes[e])

    corners = []

    def corner(half, from_prev, from_next):
        for u, copy, there in ((0, from_prev, a > 0), (2, from_next, a < 15)):
            copy.wait_recv()
            row = n.at[3 * u + 1, half]
            corners.append(
                send("cha", row, n.at[3 * u, half], next_b, there & (b < 15), there & (b > 0))
            )
            corners.append(
                send("cha", row, n.at[3 * u + 2, half], prev_b, there & (b > 0), there & (b < 15))
            )

    corner(*charges_a[0])
    across(*came_z[0])
    across(*came_z[1])
    corner(*charges_a[1])
    near_add([(0, 1), (2, 1)])
    across(*came_z[2])
    across(*came_z[3])

    quarter_c.wait_recv()
    quarter_x.wait_recv()
    other_rows = pl.ds(pl.multiple_of((2 * (1 - alpha) + c) * 32, 32), 32)
    quarter_d = send("ctg", ct.at[:, other_rows, :], ct.at[:, other_rows, :], core)
    across(*came_z[4])
    across(*came_z[5])
    for copy in charges_b:
        copy.wait_recv()
    near_add([(1, 0), (1, 2)])

    quarter_d.wait_recv()
    for copy in top_y:
        copy.wait_recv()
    quarter = None
    for s in range(SLOTS):
        big_p, big_q = place(s, xh, zp)
        vp, vq = 2 * y - 2 + big_p, 2 * zz - 2 + big_q
        inside = (vp >= 0) & (vp < 8) & (vq >= 0) & (vq < 8)
        box = t[jnp.where(inside, big_q, 6), jnp.where(inside, big_p, 0)]
        product = dot(box, ct[s], (1, 1))
        quarter = product if quarter is None else quarter + product
    lt[mine] = quarter.astype(BF16)
    siblings = [(1, 0), (1, 1), (0, 1)]
    expansion = [send("top", lt.at[mine], lt.at[mine], ring_device[k]) for k in siblings]

    load_cl.wait()
    for copy in to_core:
        copy.wait_recv()
    local_leaf = None
    for s in range(SLOTS):
        big_a, big_b = place(s, alpha, c)
        va, vb = a - alpha - 2 + big_a, b - c - 2 + big_b
        inside = (va >= 0) & (va < 16) & (vb >= 0) & (vb < 16)
        row = jnp.where(inside, (big_b % 2) * 6 + big_a, 12)
        product = dot(cl[s], w[row, jnp.where(inside, big_b // 2, 0)], (1, 0))
        local_leaf = product if local_leaf is None else local_leaf + product

    for copy in corners:
        copy.wait_recv()
    near_add([(0, 0), (0, 2), (2, 0), (2, 2)])

    for copy in expansion:
        copy.wait_recv()
    full = lt[...].reshape(NRHS, RANK)
    total = (local_leaf + dot(transfer[...], full, (1, 1))).astype(BF16)
    stores = []
    for i in range(LEAF // TILE):
        rows = pl.ds(i * TILE, TILE)
        out[rows, :] = (acc[rows, :] + dot(basis[rows, :], total, (1, 0))).astype(BF16)
        stores.append(local(out.at[rows, :], out_hbm.at[0, 0, rows, :]))

    for copy in sent:
        copy.wait_send()
    for copy in stores:
        copy.wait()


def shards(charges, near_blocks, basis, transfer, coupling_leaf, coupling_top):
    any_space = pl.BlockSpec(memory_space=pl.ANY)
    return pl.pallas_call(
        kernel,
        out_shape=jax.ShapeDtypeStruct((1, 1, LEAF, NRHS), BF16),
        in_specs=[any_space] * 6,
        out_specs=any_space,
        scratch_shapes=[
            pltpu.VMEM((3, 3, LEAF, LEAF), BF16),
            pltpu.VMEM((LEAF, RANK), BF16),
            pltpu.VMEM((RANK, RANK), BF16),
            pltpu.VMEM((SLOTS, RANK, RANK), BF16),
            pltpu.VMEM((SLOTS, RANK, RANK), BF16),
            pltpu.VMEM((10, LEAF, NRHS), BF16),
            pltpu.VMEM((13, 3, RANK, NRHS), BF16),
            pltpu.VMEM((4, PART, RANK), BF16),
            pltpu.VMEM((2, 4, PART, RANK), BF16),
            pltpu.VMEM((7, 6, PART, RANK), BF16),
            pltpu.VMEM((4, PART, RANK), BF16),
            pltpu.VMEM((LEAF, NRHS), F32),
            pltpu.VMEM((LEAF, NRHS), BF16),
            pltpu.SemaphoreType.DMA((8,)),
            pltpu.SemaphoreType.DMA((72,)),
            pltpu.SemaphoreType.DMA((72,)),
        ],
        compiler_params=pltpu.CompilerParams(
            collective_id=0, has_side_effects=True, vmem_limit_bytes=60 * 1024 * 1024
        ),
        cost_estimate=pl.CostEstimate(
            flops=1_600_000_000, bytes_accessed=6_500_000, transcendentals=0
        ),
    )(charges, near_blocks, basis, transfer, coupling_leaf, coupling_top)


def solution(mesh):
    return jax.shard_map(
        shards,
        mesh=mesh,
        in_specs=(
            P("gx", "gy", None, None),
            P("gx", "gy", None, None, None, None),
            P("gx", "gy", None, None),
            P("gx", "gy", None, None),
            P("gx", "gy", None, None, None),
            P("gx", "gy", None, None, None),
        ),
        out_specs=P("gx", "gy", None, None),
        check_vma=False,
    )
```

```python
import jax
import jax.numpy as jnp
from jax import lax
from jax.experimental import pallas as pl
from jax.experimental.pallas import tpu as pltpu
from jax.sharding import PartitionSpec as P

F32, BF16 = jnp.float32, jnp.bfloat16
SLOTS, ROWS, LEAF, NRHS, RANK = 27, 16, 512, 256, 128
PART = NRHS // 4
TILE = 256
TURN = 64


def cousin_positions():
    table = {}
    for i in range(2):
        for j in range(2):
            table[i, j] = [
                (big_a, big_b)
                for big_a in range(6)
                for big_b in range(6)
                if not (abs(big_a - 2 - i) <= 1 and abs(big_b - 2 - j) <= 1)
            ]
    return table


POSITIONS = cousin_positions()


def pick(value, i, j):
    v00, v01, v10, v11 = (value[0, 0], value[0, 1], value[1, 0], value[1, 1])
    return v00 + i * (v10 - v00) + j * (v01 - v00) + i * j * (v11 - v10 - v01 + v00)


def place(slot, i, j):
    big_a = pick({k: t[slot][0] for k, t in POSITIONS.items()}, i, j)
    big_b = pick({k: t[slot][1] for k, t in POSITIONS.items()}, i, j)
    return big_a, big_b


def dot(a, b, contract):
    return lax.dot_general(a, b, ((contract[:1], contract[1:]), ((), ())), preferred_element_type=F32)


class Copy:
    def __init__(self, make, goes, comes):
        self.make, self.goes, self.comes = make, goes, comes

    def _if(self, condition, act):
        if condition is True:
            act()
        else:
            pl.when(condition)(act)

    def start(self):
        self._if(self.goes, lambda: self.make().start())

    def wait_recv(self):
        self._if(self.comes, lambda: self.make().wait_recv())

    def wait_send(self):
        self._if(self.goes, lambda: self.make().wait_send())


def both(p, q):
    return q if p is True else p if q is True else p & q


def kernel(
    x_hbm, near_hbm, basis_hbm, transfer_hbm, leaf_hbm, top_hbm, out,
    near, basis, transfer, cl, ct, n, w, term, rb, t, lt, acc,
    local_sem, send_sem, recv_sem,
):
    a, b = lax.axis_index("gx"), lax.axis_index("gy")
    y, x = a // 4, a % 4
    z, c = b // 2, b % 2
    xh, alpha = x // 2, x % 2
    zz, zp = z // 2, z % 2
    mine = 2 * alpha + c

    def device(y, x, z, c):
        return (y * 4 + x, z * 2 + c)

    def flip(v, by):
        high, low = v // 2, v % 2
        return 2 * ((high + by // 2) % 2) + (low + by % 2) % 2

    locals_ = []

    def local(src, dst):
        copy = pltpu.make_async_copy(src, dst, local_sem.at[len(locals_)])
        copy.start()
        locals_.append(copy)
        return copy

    load_x = local(x_hbm.at[0, 0], n.at[4])
    load_basis = local(basis_hbm.at[0, 0], basis)
    load_transfer = local(transfer_hbm.at[0, 0], transfer)

    ring = [(dx, dc) for dx in (2, 1, 3, 0) for dc in range(2) if (dx, dc) != (0, 0)]
    ring_device = {k: device(y, flip(x, k[0]), z, (c + k[1]) % 2) for k in ring}
    core = ring_device[0, 1]
    up, down = y < 3, y > 0
    up_y, down_y = device((y + 1) % 4, x, z, c), device((y + 3) % 4, x, z, c)
    over = ((xh == 1) & up) | ((xh == 0) & down)
    over_device = [
        device((y + 3 + 2 * xh) % 4, flip(x, 2 + g), z, c) for g in range(2)
    ]
    window = [(0, 1), (-1, 0), (-1, 1), (1, 0), (1, 1)]
    window_device = {
        (e, g): device(y, x, 2 * ((zz + 4 + e) % 4) + (zp + g) % 2, c) for e, g in window
    }
    window_goes = {-1: zz > 0, 0: True, 1: zz < 3}
    window_comes = {-1: zz < 3, 0: True, 1: zz > 0}
    next_a, prev_a = ((a + 1) % 16, b), ((a + 15) % 16, b)
    next_b, prev_b = (a, (b + 1) % 16), (a, (b + 15) % 16)
    next_z, prev_z = device(y, x, (z + 1) % 8, c), device(y, x, (z + 7) % 8, c)
    far_b = device(y, x, (z + 7 + 2 * c) % 8, 1 - c)
    far = ((c == 1) & (z < 7)) | ((c == 0) & (z > 0))

    barrier = pltpu.get_barrier_semaphore()

    def greet(partners):
        for partner in partners:
            pl.semaphore_signal(
                barrier, inc=1, device_id=partner, device_id_type=pl.DeviceIdType.MESH
            )

    pl.when(zz > 0)(lambda: greet([window_device[-1, 0], window_device[-1, 1]]))
    pl.when(zz < 3)(lambda: greet([window_device[1, 0], window_device[1, 1]]))
    greet([window_device[0, 1]])
    pl.when(up)(lambda: greet([up_y]))
    pl.when(down)(lambda: greet([down_y]))
    pl.when(over)(lambda: greet(over_device))
    pl.when(far)(lambda: greet([far_b]))
    greet([ring_device[k] for k in ring])

    def one(condition):
        return jnp.where(condition, 1, 0)

    expected = (
        8 + 2 * one(zz > 0) + 2 * one(zz < 3) + one(up) + one(down) + 2 * one(over) + one(far)
    )

    sent = []

    def send(kind, src, dst, to, goes=True, comes=True, now=True):
        k = len(sent)
        copy = Copy(
            lambda: pltpu.make_async_remote_copy(
                src_ref=src, dst_ref=dst, send_sem=send_sem.at[k], recv_sem=recv_sem.at[k],
                device_id=to, device_id_type=pl.DeviceIdType.MESH,
            ),
            goes,
            comes,
        )
        if now:
            copy.start()
        sent.append(copy)
        return copy

    n[9] = jnp.zeros((LEAF, NRHS), BF16)
    w[12, 0] = jnp.zeros((RANK, NRHS), BF16)
    t[6, 0] = jnp.zeros((PART, RANK), BF16)

    load_x.wait()
    load_basis.wait()
    moments = dot(basis[...], n[4], (0, 0)).astype(BF16)
    own = 2 + alpha
    w[c * 6 + own, 1] = moments
    load_transfer.wait()
    my_rows = pl.ds(pl.multiple_of(mine * 32, 32), 32)
    load_ct = local(top_hbm.at[0, 0], ct.at[:, my_rows, :])
    load_near = local(near_hbm.at[0, 0], near)
    load_cl = local(leaf_hbm.at[0, 0], cl)
    terms = dot(moments, transfer[...], (0, 0)).astype(BF16)
    term[...] = terms.reshape(4, PART, RANK)
    rb[xh, mine] = term[mine]

    pl.semaphore_wait(barrier, expected)

    top_term = [
        send(
            "top",
            term.at[2 * ((alpha + dx % 2) % 2) + (c + dc) % 2],
            rb.at[xh, mine],
            ring_device[dx, dc],
        )
        for dx, dc in ring
    ]
    center = w.at[c * 6 + own, 1]
    came_from = []
    for dx in (1, 3, 2):
        far_h = (xh + dx // 2) % 2
        copy = send("mom", center, w.at[c * 6 + x + 2 * (1 - far_h), 1], ring_device[dx, 0])
        came_from.append((flip(x, dx) + 2 * (1 - xh), copy, True))
    for g in range(2):
        copy = send(
            "mom", center, w.at[c * 6 + alpha + 4 * (1 - xh), 1], over_device[g], over, over
        )
        came_from.append(((alpha + g) % 2 + 4 * xh, copy, over))

    to_core = []

    def along_z(row, there):
        place_ = c * 6 + row
        return (
            row,
            there,
            send("mom", w.at[place_, 1], w.at[place_, 0], next_z, both(there, z < 7), both(there, z > 0)),
            send("mom", w.at[place_, 1], w.at[place_, 2], prev_z, both(there, z > 0), both(there, z < 7)),
        )

    def across(row, there, from_prev, from_next):
        from_prev.wait_recv()
        from_next.wait_recv()
        place_ = c * 6 + row
        to_core.append(send("mom", w.at[place_], w.at[place_], core, there, there))

    came_z = [along_z(own, True)]

    first, *others = (
        pl.ds(0, TURN),
        pl.ds(TURN, (LEAF - TURN) // 2),
        pl.ds((LEAF + TURN) // 2, (LEAF - TURN) // 2),
    )
    rest = pl.ds(TURN, LEAF - TURN)
    side = 2 * c
    turned = send("cha", n.at[4, first], n.at[5 - side, first], far_b, far, far)
    unturned = send("cha", n.at[4, rest], n.at[5 - side, rest], far_b, far, far)
    charges_a = []

    def along_a(part):
        charges_a.append(
            (
                part,
                send("cha", n.at[4, part], n.at[1, part], next_a, a < 15, a > 0),
                send("cha", n.at[4, part], n.at[7, part], prev_a, a > 0, a < 15),
            )
        )

    for part in others:
        along_a(part)
    load_ct.wait()
    quarter_x = send("ctg", ct.at[:, my_rows, :], ct.at[:, my_rows, :], ring_device[1, 0])
    quarter_c = send("ctg", ct.at[:, my_rows, :], ct.at[:, my_rows, :], core)
    along_a(first)
    paired = send("cha", n.at[4], n.at[3 + side], core)

    def charge_at(u, v):
        va, vb = a + u - 1, b + v - 1
        inside = (va >= 0) & (va < 16) & (vb >= 0) & (vb < 16)
        return jnp.where(inside, 3 * u + v, 9)

    def near_add(blocks, first=False):
        @pl.loop(0, LEAF // TILE)
        def _(i):
            rows = pl.ds(pl.multiple_of(i * TILE, TILE), TILE)
            total = None if first else acc[rows, :]
            for u, v in blocks:
                product = dot(near[u, v, rows, :], n[charge_at(u, v)], (1, 0))
                total = product if total is None else total + product
            acc[rows, :] = total

    for copy in top_term:
        copy.wait_recv()
    for h in range(2):
        total = rb[h, 0].astype(F32)
        for j in range(1, 4):
            total = total + rb[h, j].astype(F32)
        t[2 + zp, 2 + h] = total.astype(BF16)
    top_z = {
        (e, g): send(
            "top",
            t.at[2 + zp, pl.ds(2, 2)],
            t.at[2 - 2 * e + zp, pl.ds(2, 2)],
            window_device[e, g],
            window_goes[e],
            window_comes[e],
        )
        for e, g in window
    }

    for row, copy, there in came_from:
        copy.wait_recv()
        came_z.append(along_z(row, there))

    far_corners, core_corners = [], []
    turned.wait_recv()
    row = n.at[3 + side, first]
    far_corners.append(send("cha", row, n.at[side, first], next_a, far & (a < 15), far & (a > 0)))
    far_corners.append(send("cha", row, n.at[6 + side, first], prev_a, far & (a > 0), far & (a < 15)))

    load_near.wait()
    near_add([(1, 1)], first=True)

    top_y = []

    def along_y(pair, there):
        columns = pl.ds(2 * pair, 2)
        for rows, to, goes, comes in ((0, up_y, up, down), (4, down_y, down, up)):
            top_y.append(
                send(
                    "top",
                    t.at[columns, pl.ds(2, 2)],
                    t.at[columns, pl.ds(rows, 2)],
                    to,
                    both(there, goes),
                    both(there, comes),
                )
            )

    top_z[0, 1].wait_recv()
    along_y(1, True)
    for e in (-1, 1):
        top_z[e, 0].wait_recv()
        top_z[e, 1].wait_recv()
        along_y(1 - e, window_comes[e])

    def corner(part, from_prev, from_next, over_z):
        for u, copy, there in ((0, from_prev, a > 0), (2, from_next, a < 15)):
            copy.wait_recv()
            row = n.at[3 * u + 1, part]
            if over_z:
                far_corners.append(
                    send("cha", row, n.at[3 * u + 2 - side, part], far_b, there & far, there & far)
                )
            core_corners.append(send("cha", row, n.at[3 * u + side, part], core, there, there))

    corner(*charges_a[0], True)
    across(*came_z[0])
    across(*came_z[1])
    corner(*charges_a[1], True)
    across(*came_z[2])
    across(*came_z[3])

    quarter_c.wait_recv()
    quarter_x.wait_recv()
    other_rows = pl.ds(pl.multiple_of((2 * (1 - alpha) + c) * 32, 32), 32)
    quarter_d = send("ctg", ct.at[:, other_rows, :], ct.at[:, other_rows, :], core)
    across(*came_z[4])
    across(*came_z[5])
    paired.wait_recv()
    unturned.wait_recv()
    near_add([(1, 0), (1, 2)])
    corner(*charges_a[2], False)
    near_add([(0, 1), (2, 1)])

    quarter_d.wait_recv()
    for copy in top_y:
        copy.wait_recv()
    quarter = None
    for s in range(SLOTS):
        big_p, big_q = place(s, xh, zp)
        vp, vq = 2 * y - 2 + big_p, 2 * zz - 2 + big_q
        inside = (vp >= 0) & (vp < 8) & (vq >= 0) & (vq < 8)
        box = t[jnp.where(inside, big_q, 6), jnp.where(inside, big_p, 0)]
        product = dot(box, ct[s], (1, 1))
        quarter = product if quarter is None else quarter + product
    lt[mine] = quarter.astype(BF16)
    siblings = [(1, 0), (1, 1), (0, 1)]
    expansion = [send("top", lt.at[mine], lt.at[mine], ring_device[k]) for k in siblings]

    for copy in core_corners:
        copy.wait_recv()
    near_add([(0, 2 - side), (2, 2 - side)])

    load_cl.wait()
    for copy in to_core:
        copy.wait_recv()
    local_leaf = None
    for s in range(SLOTS):
        big_a, big_b = place(s, alpha, c)
        va, vb = a - alpha - 2 + big_a, b - c - 2 + big_b
        inside = (va >= 0) & (va < 16) & (vb >= 0) & (vb < 16)
        row = jnp.where(inside, (big_b % 2) * 6 + big_a, 12)
        product = dot(cl[s], w[row, jnp.where(inside, big_b // 2, 0)], (1, 0))
        local_leaf = product if local_leaf is None else local_leaf + product

    for copy in far_corners:
        copy.wait_recv()
    near_add([(0, side), (2, side)])

    for copy in expansion:
        copy.wait_recv()
    full = lt[...].reshape(NRHS, RANK)
    total = (local_leaf + dot(transfer[...], full, (1, 1))).astype(BF16)
    for i in range(LEAF // TILE):
        rows = pl.ds(i * TILE, TILE)
        out[0, 0, rows, :] = (acc[rows, :] + dot(basis[rows, :], total, (1, 0))).astype(BF16)

    for copy in sent:
        copy.wait_send()


def shards(charges, near_blocks, basis, transfer, coupling_leaf, coupling_top):
    any_space = pl.BlockSpec(memory_space=pl.ANY)
    return pl.pallas_call(
        kernel,
        out_shape=pltpu.VMEM((1, 1, LEAF, NRHS), BF16),
        in_specs=[any_space] * 6,
        out_specs=pl.BlockSpec(memory_space=pltpu.VMEM),
        scratch_shapes=[
            pltpu.VMEM((3, 3, LEAF, LEAF), BF16),
            pltpu.VMEM((LEAF, RANK), BF16),
            pltpu.VMEM((RANK, RANK), BF16),
            pltpu.VMEM((SLOTS, RANK, RANK), BF16),
            pltpu.VMEM((SLOTS, RANK, RANK), BF16),
            pltpu.VMEM((10, LEAF, NRHS), BF16),
            pltpu.VMEM((13, 3, RANK, NRHS), BF16),
            pltpu.VMEM((4, PART, RANK), BF16),
            pltpu.VMEM((2, 4, PART, RANK), BF16),
            pltpu.VMEM((7, 6, PART, RANK), BF16),
            pltpu.VMEM((4, PART, RANK), BF16),
            pltpu.VMEM((LEAF, NRHS), F32),
            pltpu.SemaphoreType.DMA((8,)),
            pltpu.SemaphoreType.DMA((72,)),
            pltpu.SemaphoreType.DMA((72,)),
        ],
        compiler_params=pltpu.CompilerParams(
            collective_id=0, has_side_effects=True, vmem_limit_bytes=60 * 1024 * 1024
        ),
        cost_estimate=pl.CostEstimate(
            flops=1_600_000_000, bytes_accessed=6_500_000, transcendentals=0
        ),
    )(charges, near_blocks, basis, transfer, coupling_leaf, coupling_top)


def solution(mesh):
    return jax.shard_map(
        shards,
        mesh=mesh,
        in_specs=(
            P("gx", "gy", None, None),
            P("gx", "gy", None, None, None, None),
            P("gx", "gy", None, None),
            P("gx", "gy", None, None),
            P("gx", "gy", None, None, None),
            P("gx", "gy", None, None, None),
        ),
        out_specs=P("gx", "gy", None, None),
        check_vma=False,
    )
```

```python
import jax
import jax.numpy as jnp
from jax import lax
from jax.experimental import pallas as pl
from jax.experimental.pallas import tpu as pltpu
from jax.sharding import PartitionSpec as P

F32, BF16 = jnp.float32, jnp.bfloat16
SLOTS, ROWS, LEAF, NRHS, RANK = 27, 16, 512, 256, 128
PART = NRHS // 4
TILE = 256
TURN = 64


def cousin_positions():
    table = {}
    for i in range(2):
        for j in range(2):
            table[i, j] = [
                (big_a, big_b)
                for big_a in range(6)
                for big_b in range(6)
                if not (abs(big_a - 2 - i) <= 1 and abs(big_b - 2 - j) <= 1)
            ]
    return table


POSITIONS = cousin_positions()


def pick(value, i, j):
    v00, v01, v10, v11 = (value[0, 0], value[0, 1], value[1, 0], value[1, 1])
    return v00 + i * (v10 - v00) + j * (v01 - v00) + i * j * (v11 - v10 - v01 + v00)


def place(slot, i, j):
    big_a = pick({k: t[slot][0] for k, t in POSITIONS.items()}, i, j)
    big_b = pick({k: t[slot][1] for k, t in POSITIONS.items()}, i, j)
    return big_a, big_b


def dot(a, b, contract):
    return lax.dot_general(a, b, ((contract[:1], contract[1:]), ((), ())), preferred_element_type=F32)


class Copy:
    def __init__(self, make, goes, comes):
        self.make, self.goes, self.comes = make, goes, comes

    def _if(self, condition, act):
        if condition is True:
            act()
        else:
            pl.when(condition)(act)

    def start(self):
        self._if(self.goes, lambda: self.make().start())

    def wait_recv(self):
        self._if(self.comes, lambda: self.make().wait_recv())

    def wait_send(self):
        self._if(self.goes, lambda: self.make().wait_send())


def both(p, q):
    return q if p is True else p if q is True else p & q


def kernel(
    x_hbm, near_hbm, basis_hbm, transfer_hbm, leaf_hbm, top_hbm, out,
    near, basis, transfer, cl, ct, n, w, term, rb, t, lt, acc,
    local_sem, send_sem, recv_sem, known_sem,
):
    a, b = lax.axis_index("gx"), lax.axis_index("gy")
    y, x = a // 4, a % 4
    z, c = b // 2, b % 2
    xh, alpha = x // 2, x % 2
    zz, zp = z // 2, z % 2
    mine = 2 * alpha + c

    def device(y, x, z, c):
        return (y * 4 + x, z * 2 + c)

    def flip(v, by):
        high, low = v // 2, v % 2
        return 2 * ((high + by // 2) % 2) + (low + by % 2) % 2

    locals_ = []

    def local(src, dst):
        copy = pltpu.make_async_copy(src, dst, local_sem.at[len(locals_)])
        copy.start()
        locals_.append(copy)
        return copy

    load_x = local(x_hbm.at[0, 0], n.at[4])
    load_basis = local(basis_hbm.at[0, 0], basis)
    load_transfer = local(transfer_hbm.at[0, 0], transfer)

    ring = [(dx, dc) for dx in (2, 1, 3, 0) for dc in range(2) if (dx, dc) != (0, 0)]
    ring_device = {k: device(y, flip(x, k[0]), z, (c + k[1]) % 2) for k in ring}
    core = ring_device[0, 1]
    up, down = y < 3, y > 0
    up_y, down_y = device((y + 1) % 4, x, z, c), device((y + 3) % 4, x, z, c)
    over = ((xh == 1) & up) | ((xh == 0) & down)
    over_device = [
        device((y + 3 + 2 * xh) % 4, flip(x, 2 + g), z, c) for g in range(2)
    ]
    window = [(0, 1), (-1, 0), (-1, 1), (1, 0), (1, 1)]
    window_device = {
        (e, g): device(y, x, 2 * ((zz + 4 + e) % 4) + (zp + g) % 2, c) for e, g in window
    }
    window_goes = {-1: zz > 0, 0: True, 1: zz < 3}
    window_comes = {-1: zz < 3, 0: True, 1: zz > 0}
    next_a, prev_a = ((a + 1) % 16, b), ((a + 15) % 16, b)
    next_b, prev_b = (a, (b + 1) % 16), (a, (b + 15) % 16)
    next_z, prev_z = device(y, x, (z + 1) % 8, c), device(y, x, (z + 7) % 8, c)
    far_b = device(y, x, (z + 7 + 2 * c) % 8, 1 - c)
    far = ((c == 1) & (z < 7)) | ((c == 0) & (z > 0))

    barrier = pltpu.get_barrier_semaphore()

    def greet(partners):
        for partner in partners:
            pl.semaphore_signal(
                barrier, inc=1, device_id=partner, device_id_type=pl.DeviceIdType.MESH
            )

    pl.when(z > 0)(lambda: greet([prev_z]))
    pl.when(z < 7)(lambda: greet([next_z]))
    pl.when(up)(lambda: greet([up_y]))
    pl.when(down)(lambda: greet([down_y]))
    pl.when(over)(lambda: greet(over_device))
    pl.when(far)(lambda: greet([far_b]))
    greet([ring_device[k] for k in ring])

    def one(condition):
        return jnp.where(condition, 1, 0)

    expected = (
        7 + one(z > 0) + one(z < 7) + one(up) + one(down) + 2 * one(over) + one(far)
    )

    sent = []

    def send(kind, src, dst, to, goes=True, comes=True, now=True):
        k = len(sent)
        copy = Copy(
            lambda: pltpu.make_async_remote_copy(
                src_ref=src, dst_ref=dst, send_sem=send_sem.at[k], recv_sem=recv_sem.at[k],
                device_id=to, device_id_type=pl.DeviceIdType.MESH,
            ),
            goes,
            comes,
        )
        if now:
            copy.start()
        sent.append(copy)
        return copy

    n[9] = jnp.zeros((LEAF, NRHS), BF16)
    w[12, 0] = jnp.zeros((RANK, NRHS), BF16)
    t[6, 0] = jnp.zeros((PART, RANK), BF16)

    load_x.wait()
    load_basis.wait()
    moments = dot(basis[...], n[4], (0, 0)).astype(BF16)
    own = 2 + alpha
    w[c * 6 + own, 1] = moments
    load_transfer.wait()
    my_rows = pl.ds(pl.multiple_of(mine * 32, 32), 32)
    load_ct = local(top_hbm.at[0, 0], ct.at[:, my_rows, :])
    load_near = local(near_hbm.at[0, 0], near)
    load_cl = local(leaf_hbm.at[0, 0], cl)
    terms = dot(moments, transfer[...], (0, 0)).astype(BF16)
    term[...] = terms.reshape(4, PART, RANK)
    rb[xh, mine] = term[mine]

    pl.semaphore_wait(barrier, expected)

    top_term = [
        send(
            "top",
            term.at[2 * ((alpha + dx % 2) % 2) + (c + dc) % 2],
            rb.at[xh, mine],
            ring_device[dx, dc],
        )
        for dx, dc in ring
    ]
    center = w.at[c * 6 + own, 1]
    came_from = []
    for dx in (1, 3, 2):
        far_h = (xh + dx // 2) % 2
        copy = send("mom", center, w.at[c * 6 + x + 2 * (1 - far_h), 1], ring_device[dx, 0])
        came_from.append((flip(x, dx) + 2 * (1 - xh), copy, True))
    for g in range(2):
        copy = send(
            "mom", center, w.at[c * 6 + alpha + 4 * (1 - xh), 1], over_device[g], over, over
        )
        came_from.append(((alpha + g) % 2 + 4 * xh, copy, over))

    to_core = []

    def along_z(row, there):
        place_ = c * 6 + row
        return (
            row,
            there,
            send("mom", w.at[place_, 1], w.at[place_, 0], next_z, both(there, z < 7), both(there, z > 0)),
            send("mom", w.at[place_, 1], w.at[place_, 2], prev_z, both(there, z > 0), both(there, z < 7)),
        )

    def across(row, there, from_prev, from_next):
        if row is not own:
            from_prev.wait_recv()
            from_next.wait_recv()
        place_ = c * 6 + row
        to_core.append(send("mom", w.at[place_], w.at[place_], core, there, there))

    came_z = [along_z(own, True)]

    first, *others = (
        pl.ds(0, TURN),
        pl.ds(TURN, (LEAF - TURN) // 2),
        pl.ds((LEAF + TURN) // 2, (LEAF - TURN) // 2),
    )
    rest = pl.ds(TURN, LEAF - TURN)
    side = 2 * c
    turned = send("cha", n.at[4, first], n.at[5 - side, first], far_b, far, far)
    unturned = send("cha", n.at[4, rest], n.at[5 - side, rest], far_b, far, far)
    charges_a = []

    def along_a(part):
        charges_a.append(
            (
                part,
                send("cha", n.at[4, part], n.at[1, part], next_a, a < 15, a > 0),
                send("cha", n.at[4, part], n.at[7, part], prev_a, a > 0, a < 15),
            )
        )

    for part in others:
        along_a(part)
    load_ct.wait()
    quarter_x = send("ctg", ct.at[:, my_rows, :], ct.at[:, my_rows, :], ring_device[1, 0])
    quarter_c = send("ctg", ct.at[:, my_rows, :], ct.at[:, my_rows, :], core)
    along_a(first)
    paired = send("cha", n.at[4], n.at[3 + side], core)

    def charge_at(u, v):
        va, vb = a + u - 1, b + v - 1
        inside = (va >= 0) & (va < 16) & (vb >= 0) & (vb < 16)
        return jnp.where(inside, 3 * u + v, 9)

    def near_add(blocks, first=False):
        @pl.loop(0, LEAF // TILE)
        def _(i):
            rows = pl.ds(pl.multiple_of(i * TILE, TILE), TILE)
            total = None if first else acc[rows, :]
            for u, v in blocks:
                product = dot(near[u, v, rows, :], n[charge_at(u, v)], (1, 0))
                total = product if total is None else total + product
            acc[rows, :] = total

    for copy in top_term:
        copy.wait_recv()
    for h in range(2):
        total = rb[h, 0].astype(F32)
        for j in range(1, 4):
            total = total + rb[h, j].astype(F32)
        t[2 + zp, 2 + h] = total.astype(BF16)
    for copy in came_z[0][2:]:
        copy.wait_recv()
    pair = window_device[0, 1]
    pl.when(((zp == 1) & (zz < 3)) | ((zp == 0) & (zz > 0)))(
        lambda: pl.semaphore_signal(
            known_sem, inc=1, device_id=pair, device_id_type=pl.DeviceIdType.MESH
        )
    )
    pl.when(((zp == 0) & (zz < 3)) | ((zp == 1) & (zz > 0)))(
        lambda: pl.semaphore_wait(known_sem, 1)
    )
    top_z = {
        (e, g): send(
            "top",
            t.at[2 + zp, pl.ds(2, 2)],
            t.at[2 - 2 * e + zp, pl.ds(2, 2)],
            window_device[e, g],
            window_goes[e],
            window_comes[e],
        )
        for e, g in window
    }

    for row, copy, there in came_from:
        copy.wait_recv()
        came_z.append(along_z(row, there))

    far_corners, core_corners = [], []
    turned.wait_recv()
    row = n.at[3 + side, first]
    far_corners.append(send("cha", row, n.at[side, first], next_a, far & (a < 15), far & (a > 0)))
    far_corners.append(send("cha", row, n.at[6 + side, first], prev_a, far & (a > 0), far & (a < 15)))

    load_near.wait()
    near_add([(1, 1)], first=True)

    top_y = []

    def along_y(pair, there):
        columns = pl.ds(2 * pair, 2)
        for rows, to, goes, comes in ((0, up_y, up, down), (4, down_y, down, up)):
            top_y.append(
                send(
                    "top",
                    t.at[columns, pl.ds(2, 2)],
                    t.at[columns, pl.ds(rows, 2)],
                    to,
                    both(there, goes),
                    both(there, comes),
                )
            )

    top_z[0, 1].wait_recv()
    along_y(1, True)
    for e in (-1, 1):
        top_z[e, 0].wait_recv()
        top_z[e, 1].wait_recv()
        along_y(1 - e, window_comes[e])

    def corner(part, from_prev, from_next, over_z):
        for u, copy, there in ((0, from_prev, a > 0), (2, from_next, a < 15)):
            copy.wait_recv()
            row = n.at[3 * u + 1, part]
            if over_z:
                far_corners.append(
                    send("cha", row, n.at[3 * u + 2 - side, part], far_b, there & far, there & far)
                )
            core_corners.append(send("cha", row, n.at[3 * u + side, part], core, there, there))

    corner(*charges_a[0], True)
    across(*came_z[0])
    across(*came_z[1])
    corner(*charges_a[1], True)
    across(*came_z[2])
    across(*came_z[3])

    quarter_c.wait_recv()
    quarter_x.wait_recv()
    other_rows = pl.ds(pl.multiple_of((2 * (1 - alpha) + c) * 32, 32), 32)
    quarter_d = send("ctg", ct.at[:, other_rows, :], ct.at[:, other_rows, :], core)
    across(*came_z[4])
    across(*came_z[5])
    paired.wait_recv()
    unturned.wait_recv()
    near_add([(1, 0), (1, 2)])
    corner(*charges_a[2], False)
    near_add([(0, 1), (2, 1)])

    quarter_d.wait_recv()
    for copy in top_y:
        copy.wait_recv()
    quarter = None
    for s in range(SLOTS):
        big_p, big_q = place(s, xh, zp)
        vp, vq = 2 * y - 2 + big_p, 2 * zz - 2 + big_q
        inside = (vp >= 0) & (vp < 8) & (vq >= 0) & (vq < 8)
        box = t[jnp.where(inside, big_q, 6), jnp.where(inside, big_p, 0)]
        product = dot(box, ct[s], (1, 1))
        quarter = product if quarter is None else quarter + product
    lt[mine] = quarter.astype(BF16)
    siblings = [(1, 0), (1, 1), (0, 1)]
    expansion = [send("top", lt.at[mine], lt.at[mine], ring_device[k]) for k in siblings]

    for copy in core_corners:
        copy.wait_recv()
    near_add([(0, 2 - side), (2, 2 - side)])

    load_cl.wait()
    for copy in to_core:
        copy.wait_recv()
    local_leaf = None
    for s in range(SLOTS):
        big_a, big_b = place(s, alpha, c)
        va, vb = a - alpha - 2 + big_a, b - c - 2 + big_b
        inside = (va >= 0) & (va < 16) & (vb >= 0) & (vb < 16)
        row = jnp.where(inside, (big_b % 2) * 6 + big_a, 12)
        product = dot(cl[s], w[row, jnp.where(inside, big_b // 2, 0)], (1, 0))
        local_leaf = product if local_leaf is None else local_leaf + product

    for copy in expansion:
        copy.wait_recv()
    full = lt[...].reshape(NRHS, RANK)
    total = (local_leaf + dot(transfer[...], full, (1, 1))).astype(BF16)
    for copy in far_corners:
        copy.wait_recv()
    for i in range(LEAF // TILE):
        rows = pl.ds(i * TILE, TILE)
        result = acc[rows, :] + dot(basis[rows, :], total, (1, 0))
        for u in (0, 2):
            result = result + dot(near[u, side, rows, :], n[charge_at(u, side)], (1, 0))
        out[0, 0, rows, :] = result.astype(BF16)

    for copy in sent:
        copy.wait_send()


def shards(charges, near_blocks, basis, transfer, coupling_leaf, coupling_top):
    any_space = pl.BlockSpec(memory_space=pl.ANY)
    return pl.pallas_call(
        kernel,
        out_shape=pltpu.VMEM((1, 1, LEAF, NRHS), BF16),
        in_specs=[any_space] * 6,
        out_specs=pl.BlockSpec(memory_space=pltpu.VMEM),
        scratch_shapes=[
            pltpu.VMEM((3, 3, LEAF, LEAF), BF16),
            pltpu.VMEM((LEAF, RANK), BF16),
            pltpu.VMEM((RANK, RANK), BF16),
            pltpu.VMEM((SLOTS, RANK, RANK), BF16),
            pltpu.VMEM((SLOTS, RANK, RANK), BF16),
            pltpu.VMEM((10, LEAF, NRHS), BF16),
            pltpu.VMEM((13, 3, RANK, NRHS), BF16),
            pltpu.VMEM((4, PART, RANK), BF16),
            pltpu.VMEM((2, 4, PART, RANK), BF16),
            pltpu.VMEM((7, 6, PART, RANK), BF16),
            pltpu.VMEM((4, PART, RANK), BF16),
            pltpu.VMEM((LEAF, NRHS), F32),
            pltpu.SemaphoreType.DMA((8,)),
            pltpu.SemaphoreType.DMA((96,)),
            pltpu.SemaphoreType.DMA((96,)),
            pltpu.SemaphoreType.REGULAR,
        ],
        compiler_params=pltpu.CompilerParams(
            collective_id=0, has_side_effects=True, vmem_limit_bytes=60 * 1024 * 1024
        ),
        cost_estimate=pl.CostEstimate(
            flops=1_600_000_000, bytes_accessed=6_500_000, transcendentals=0
        ),
    )(charges, near_blocks, basis, transfer, coupling_leaf, coupling_top)


def solution(mesh):
    return jax.shard_map(
        shards,
        mesh=mesh,
        in_specs=(
            P("gx", "gy", None, None),
            P("gx", "gy", None, None, None, None),
            P("gx", "gy", None, None),
            P("gx", "gy", None, None),
            P("gx", "gy", None, None, None),
            P("gx", "gy", None, None, None),
        ),
        out_specs=P("gx", "gy", None, None),
        check_vma=False,
    )
```

```python
import jax
import jax.numpy as jnp
from jax import lax
from jax.experimental import pallas as pl
from jax.experimental.pallas import tpu as pltpu
from jax.sharding import PartitionSpec as P

F32, BF16 = jnp.float32, jnp.bfloat16
SLOTS, ROWS, LEAF, NRHS, RANK = 27, 16, 512, 256, 128
PART = NRHS // 4
TILE = 256
TURN = 64


def cousin_positions():
    table = {}
    for i in range(2):
        for j in range(2):
            table[i, j] = [
                (big_a, big_b)
                for big_a in range(6)
                for big_b in range(6)
                if not (abs(big_a - 2 - i) <= 1 and abs(big_b - 2 - j) <= 1)
            ]
    return table


POSITIONS = cousin_positions()


def pick(value, i, j):
    v00, v01, v10, v11 = (value[0, 0], value[0, 1], value[1, 0], value[1, 1])
    return v00 + i * (v10 - v00) + j * (v01 - v00) + i * j * (v11 - v10 - v01 + v00)


def place(slot, i, j):
    big_a = pick({k: t[slot][0] for k, t in POSITIONS.items()}, i, j)
    big_b = pick({k: t[slot][1] for k, t in POSITIONS.items()}, i, j)
    return big_a, big_b


def dot(a, b, contract):
    return lax.dot_general(a, b, ((contract[:1], contract[1:]), ((), ())), preferred_element_type=F32)


class Copy:
    def __init__(self, make, goes, comes):
        self.make, self.goes, self.comes = make, goes, comes

    def _if(self, condition, act):
        if condition is True:
            act()
        else:
            pl.when(condition)(act)

    def start(self):
        self._if(self.goes, lambda: self.make().start())

    def wait_recv(self):
        self._if(self.comes, lambda: self.make().wait_recv())

    def wait_send(self):
        self._if(self.goes, lambda: self.make().wait_send())


def both(p, q):
    return q if p is True else p if q is True else p & q


def kernel(
    x_hbm, near_hbm, basis_hbm, transfer_hbm, leaf_hbm, top_hbm, out,
    near, basis, transfer, cl, ct, n, w, term, rb, t, lt, acc,
    local_sem, send_sem, recv_sem, known_sem,
):
    a, b = lax.axis_index("gx"), lax.axis_index("gy")
    y, x = a // 4, a % 4
    z, c = b // 2, b % 2
    xh, alpha = x // 2, x % 2
    zz, zp = z // 2, z % 2
    mine = 2 * alpha + c

    def device(y, x, z, c):
        return (y * 4 + x, z * 2 + c)

    def flip(v, by):
        high, low = v // 2, v % 2
        return 2 * ((high + by // 2) % 2) + (low + by % 2) % 2

    locals_ = []

    def local(src, dst):
        copy = pltpu.make_async_copy(src, dst, local_sem.at[len(locals_)])
        copy.start()
        locals_.append(copy)
        return copy

    load_x = local(x_hbm.at[0, 0], n.at[4])
    load_basis = local(basis_hbm.at[0, 0], basis)
    load_transfer = local(transfer_hbm.at[0, 0], transfer)

    ring = [(dx, dc) for dx in (2, 1, 3, 0) for dc in range(2) if (dx, dc) != (0, 0)]
    ring_device = {k: device(y, flip(x, k[0]), z, (c + k[1]) % 2) for k in ring}
    core = ring_device[0, 1]
    up, down = y < 3, y > 0
    up_y, down_y = device((y + 1) % 4, x, z, c), device((y + 3) % 4, x, z, c)
    over = ((xh == 1) & up) | ((xh == 0) & down)
    over_device = [
        device((y + 3 + 2 * xh) % 4, flip(x, 2 + g), z, c) for g in range(2)
    ]
    window = [(0, 1), (-1, 0), (-1, 1), (1, 0), (1, 1)]
    window_device = {
        (e, g): device(y, x, 2 * ((zz + 4 + e) % 4) + (zp + g) % 2, c) for e, g in window
    }
    window_goes = {-1: zz > 0, 0: True, 1: zz < 3}
    window_comes = {-1: zz < 3, 0: True, 1: zz > 0}
    next_a, prev_a = ((a + 1) % 16, b), ((a + 15) % 16, b)
    next_b, prev_b = (a, (b + 1) % 16), (a, (b + 15) % 16)
    next_z, prev_z = device(y, x, (z + 1) % 8, c), device(y, x, (z + 7) % 8, c)
    far_b = device(y, x, (z + 7 + 2 * c) % 8, 1 - c)
    far = ((c == 1) & (z < 7)) | ((c == 0) & (z > 0))

    barrier = pltpu.get_barrier_semaphore()

    def greet(partners):
        for partner in partners:
            pl.semaphore_signal(
                barrier, inc=1, device_id=partner, device_id_type=pl.DeviceIdType.MESH
            )

    pl.when(z > 0)(lambda: greet([prev_z]))
    pl.when(z < 7)(lambda: greet([next_z]))
    pl.when(up)(lambda: greet([up_y]))
    pl.when(down)(lambda: greet([down_y]))
    pl.when(over)(lambda: greet(over_device))
    pl.when(far)(lambda: greet([far_b]))
    greet([ring_device[k] for k in ring])

    def one(condition):
        return jnp.where(condition, 1, 0)

    expected = (
        7 + one(z > 0) + one(z < 7) + one(up) + one(down) + 2 * one(over) + one(far)
    )

    sent = []

    def send(kind, src, dst, to, goes=True, comes=True, now=True):
        k = len(sent)
        copy = Copy(
            lambda: pltpu.make_async_remote_copy(
                src_ref=src, dst_ref=dst, send_sem=send_sem.at[k], recv_sem=recv_sem.at[k],
                device_id=to, device_id_type=pl.DeviceIdType.MESH,
            ),
            goes,
            comes,
        )
        if now:
            copy.start()
        sent.append(copy)
        return copy

    n[9] = jnp.zeros((LEAF, NRHS), BF16)
    w[12, 0] = jnp.zeros((RANK, NRHS), BF16)
    t[6, 0] = jnp.zeros((PART, RANK), BF16)

    load_x.wait()
    load_basis.wait()
    moments = dot(basis[...], n[4], (0, 0)).astype(BF16)
    own = 2 + alpha
    w[c * 6 + own, 1] = moments
    load_transfer.wait()
    my_rows = pl.ds(pl.multiple_of(mine * 32, 32), 32)
    load_ct = local(top_hbm.at[0, 0], ct.at[:, my_rows, :])
    load_near = local(near_hbm.at[0, 0], near)
    load_cl = local(leaf_hbm.at[0, 0], cl)
    terms = dot(moments, transfer[...], (0, 0)).astype(BF16)
    term[...] = terms.reshape(4, PART, RANK)
    rb[xh, mine] = term[mine]

    pl.semaphore_wait(barrier, expected)

    top_term = [
        send(
            "top",
            term.at[2 * ((alpha + dx % 2) % 2) + (c + dc) % 2],
            rb.at[xh, mine],
            ring_device[dx, dc],
        )
        for dx, dc in ring
    ]
    center = w.at[c * 6 + own, 1]
    came_from = []
    for dx in (1, 3, 2):
        far_h = (xh + dx // 2) % 2
        copy = send("mom", center, w.at[c * 6 + x + 2 * (1 - far_h), 1], ring_device[dx, 0])
        came_from.append((flip(x, dx) + 2 * (1 - xh), copy, True))
    for g in range(2):
        copy = send(
            "mom", center, w.at[c * 6 + alpha + 4 * (1 - xh), 1], over_device[g], over, over
        )
        came_from.append(((alpha + g) % 2 + 4 * xh, copy, over))

    to_core = []

    def along_z(row, there):
        place_ = c * 6 + row
        return (
            row,
            there,
            send("mom", w.at[place_, 1], w.at[place_, 0], next_z, both(there, z < 7), both(there, z > 0)),
            send("mom", w.at[place_, 1], w.at[place_, 2], prev_z, both(there, z > 0), both(there, z < 7)),
        )

    def across(row, there, from_prev, from_next):
        if row is not own:
            from_prev.wait_recv()
            from_next.wait_recv()
        place_ = c * 6 + row
        to_core.append(send("mom", w.at[place_], w.at[place_], core, there, there))

    came_z = [along_z(own, True)]

    first, *others = (
        pl.ds(0, TURN),
        pl.ds(TURN, (LEAF - TURN) // 2),
        pl.ds((LEAF + TURN) // 2, (LEAF - TURN) // 2),
    )
    rest = pl.ds(TURN, LEAF - TURN)
    side = 2 * c
    turned = send("cha", n.at[4, first], n.at[5 - side, first], far_b, far, far)
    unturned = send("cha", n.at[4, rest], n.at[5 - side, rest], far_b, far, far)
    charges_a = []

    def along_a(part):
        charges_a.append(
            (
                part,
                send("cha", n.at[4, part], n.at[1, part], next_a, a < 15, a > 0),
                send("cha", n.at[4, part], n.at[7, part], prev_a, a > 0, a < 15),
            )
        )

    for part in others:
        along_a(part)
    load_ct.wait()
    quarter_x = send("ctg", ct.at[:, my_rows, :], ct.at[:, my_rows, :], ring_device[1, 0])
    quarter_c = send("ctg", ct.at[:, my_rows, :], ct.at[:, my_rows, :], core)
    along_a(first)
    paired = send("cha", n.at[4], n.at[3 + side], core)

    def charge_at(u, v):
        va, vb = a + u - 1, b + v - 1
        inside = (va >= 0) & (va < 16) & (vb >= 0) & (vb < 16)
        return jnp.where(inside, 3 * u + v, 9)

    def near_add(blocks, first=False):
        @pl.loop(0, LEAF // TILE)
        def _(i):
            rows = pl.ds(pl.multiple_of(i * TILE, TILE), TILE)
            total = None if first else acc[rows, :]
            for u, v in blocks:
                product = dot(near[u, v, rows, :], n[charge_at(u, v)], (1, 0))
                total = product if total is None else total + product
            acc[rows, :] = total

    for copy in came_z[0][2:]:
        copy.wait_recv()
    pair = window_device[0, 1]
    pl.when(((zp == 1) & (zz < 3)) | ((zp == 0) & (zz > 0)))(
        lambda: pl.semaphore_signal(
            known_sem, inc=1, device_id=pair, device_id_type=pl.DeviceIdType.MESH
        )
    )

    for copy in top_term:
        copy.wait_recv()
    for h in range(2):
        total = rb[h, 0].astype(F32)
        for j in range(1, 4):
            total = total + rb[h, j].astype(F32)
        t[2 + zp, 2 + h] = total.astype(BF16)
    pl.when(((zp == 0) & (zz < 3)) | ((zp == 1) & (zz > 0)))(
        lambda: pl.semaphore_wait(known_sem, 1)
    )
    top_z = {
        (e, g): send(
            "top",
            t.at[2 + zp, pl.ds(2, 2)],
            t.at[2 - 2 * e + zp, pl.ds(2, 2)],
            window_device[e, g],
            window_goes[e],
            window_comes[e],
        )
        for e, g in window
    }

    for row, copy, there in came_from:
        copy.wait_recv()
        came_z.append(along_z(row, there))

    far_corners, core_corners = [], []
    turned.wait_recv()
    row = n.at[3 + side, first]
    far_corners.append(send("cha", row, n.at[side, first], next_a, far & (a < 15), far & (a > 0)))
    far_corners.append(send("cha", row, n.at[6 + side, first], prev_a, far & (a > 0), far & (a < 15)))

    load_near.wait()
    near_add([(1, 1)], first=True)

    top_y = []

    def along_y(pair, there):
        columns = pl.ds(2 * pair, 2)
        for rows, to, goes, comes in ((0, up_y, up, down), (4, down_y, down, up)):
            top_y.append(
                send(
                    "top",
                    t.at[columns, pl.ds(2, 2)],
                    t.at[columns, pl.ds(rows, 2)],
                    to,
                    both(there, goes),
                    both(there, comes),
                )
            )

    top_z[0, 1].wait_recv()
    along_y(1, True)
    for e in (-1, 1):
        top_z[e, 0].wait_recv()
        top_z[e, 1].wait_recv()
        along_y(1 - e, window_comes[e])

    def corner(part, from_prev, from_next, over_z):
        for u, copy, there in ((0, from_prev, a > 0), (2, from_next, a < 15)):
            copy.wait_recv()
            row = n.at[3 * u + 1, part]
            if over_z:
                far_corners.append(
                    send("cha", row, n.at[3 * u + 2 - side, part], far_b, there & far, there & far)
                )
            core_corners.append(send("cha", row, n.at[3 * u + side, part], core, there, there))

    corner(*charges_a[0], True)
    across(*came_z[0])
    across(*came_z[1])
    corner(*charges_a[1], True)
    across(*came_z[2])
    across(*came_z[3])

    quarter_c.wait_recv()
    quarter_x.wait_recv()
    other_rows = pl.ds(pl.multiple_of((2 * (1 - alpha) + c) * 32, 32), 32)
    quarter_d = send("ctg", ct.at[:, other_rows, :], ct.at[:, other_rows, :], core)
    across(*came_z[4])
    across(*came_z[5])
    paired.wait_recv()
    unturned.wait_recv()
    near_add([(1, 0), (1, 2)])
    corner(*charges_a[2], False)
    near_add([(0, 1), (2, 1)])

    quarter_d.wait_recv()
    for copy in top_y:
        copy.wait_recv()
    quarter = None
    for s in range(SLOTS):
        big_p, big_q = place(s, xh, zp)
        vp, vq = 2 * y - 2 + big_p, 2 * zz - 2 + big_q
        inside = (vp >= 0) & (vp < 8) & (vq >= 0) & (vq < 8)
        box = t[jnp.where(inside, big_q, 6), jnp.where(inside, big_p, 0)]
        product = dot(box, ct[s], (1, 1))
        quarter = product if quarter is None else quarter + product
    lt[mine] = quarter.astype(BF16)
    siblings = [(1, 0), (1, 1), (0, 1)]
    expansion = [send("top", lt.at[mine], lt.at[mine], ring_device[k]) for k in siblings]

    for copy in core_corners:
        copy.wait_recv()
    near_add([(0, 2 - side), (2, 2 - side)])

    load_cl.wait()
    for copy in to_core:
        copy.wait_recv()
    local_leaf = None
    for s in range(SLOTS):
        big_a, big_b = place(s, alpha, c)
        va, vb = a - alpha - 2 + big_a, b - c - 2 + big_b
        inside = (va >= 0) & (va < 16) & (vb >= 0) & (vb < 16)
        row = jnp.where(inside, (big_b % 2) * 6 + big_a, 12)
        product = dot(cl[s], w[row, jnp.where(inside, big_b // 2, 0)], (1, 0))
        local_leaf = product if local_leaf is None else local_leaf + product

    for copy in expansion:
        copy.wait_recv()
    full = lt[...].reshape(NRHS, RANK)
    total = (local_leaf + dot(transfer[...], full, (1, 1))).astype(BF16)
    for copy in far_corners:
        copy.wait_recv()
    for i in range(LEAF // TILE):
        rows = pl.ds(i * TILE, TILE)
        result = acc[rows, :] + dot(basis[rows, :], total, (1, 0))
        for u in (0, 2):
            result = result + dot(near[u, side, rows, :], n[charge_at(u, side)], (1, 0))
        out[0, 0, rows, :] = result.astype(BF16)

    for copy in sent:
        copy.wait_send()


def shards(charges, near_blocks, basis, transfer, coupling_leaf, coupling_top):
    any_space = pl.BlockSpec(memory_space=pl.ANY)
    return pl.pallas_call(
        kernel,
        out_shape=pltpu.VMEM((1, 1, LEAF, NRHS), BF16),
        in_specs=[any_space] * 6,
        out_specs=pl.BlockSpec(memory_space=pltpu.VMEM),
        scratch_shapes=[
            pltpu.VMEM((3, 3, LEAF, LEAF), BF16),
            pltpu.VMEM((LEAF, RANK), BF16),
            pltpu.VMEM((RANK, RANK), BF16),
            pltpu.VMEM((SLOTS, RANK, RANK), BF16),
            pltpu.VMEM((SLOTS, RANK, RANK), BF16),
            pltpu.VMEM((10, LEAF, NRHS), BF16),
            pltpu.VMEM((13, 3, RANK, NRHS), BF16),
            pltpu.VMEM((4, PART, RANK), BF16),
            pltpu.VMEM((2, 4, PART, RANK), BF16),
            pltpu.VMEM((7, 6, PART, RANK), BF16),
            pltpu.VMEM((4, PART, RANK), BF16),
            pltpu.VMEM((LEAF, NRHS), F32),
            pltpu.SemaphoreType.DMA((8,)),
            pltpu.SemaphoreType.DMA((96,)),
            pltpu.SemaphoreType.DMA((96,)),
            pltpu.SemaphoreType.REGULAR,
        ],
        compiler_params=pltpu.CompilerParams(
            collective_id=0, has_side_effects=True, vmem_limit_bytes=60 * 1024 * 1024
        ),
        cost_estimate=pl.CostEstimate(
            flops=1_600_000_000, bytes_accessed=6_500_000, transcendentals=0
        ),
    )(charges, near_blocks, basis, transfer, coupling_leaf, coupling_top)


def solution(mesh):
    return jax.shard_map(
        shards,
        mesh=mesh,
        in_specs=(
            P("gx", "gy", None, None),
            P("gx", "gy", None, None, None, None),
            P("gx", "gy", None, None),
            P("gx", "gy", None, None),
            P("gx", "gy", None, None, None),
            P("gx", "gy", None, None, None),
        ),
        out_specs=P("gx", "gy", None, None),
        check_vma=False,
    )
```
